256 devices in a mesh: ctx: 128 (over y_lo, x, z, core), tp: 2 (over y_hi).
Axes of the slice: x: 4, y: 4 (y_hi: 2, y_lo: 2; y = y_hi * 2 + y_lo), z: 8, core: 2. Of those that a mesh axis runs over, the one named last changes fastest.
Arguments:
- post_gate: bfloat16 [16384, 2048], P('ctx', 'tp'), may hold values from -6 to 6
- pre_gate: bfloat16 [16384, 2048], P('ctx', 'tp'), may hold values from -6 to 6
- features: bfloat16 [16384, 2048], P('ctx', 'tp'), may hold values from -6 to 6
- filters: float32 [16384, 2048], P('ctx', 'tp'), may hold values from -1.1 to 1.1
- token_ids: int32 [16384], P('ctx'), may hold values from 0 to 5
- out_weight: bfloat16 [2048, 2048], P('tp'), may hold values from -0.125 to 0.125
- out_grad: bfloat16 [16384, 2048], P('ctx', 'tp'), may hold values from -6 to 6
Outputs:
- output: bfloat16 [16384, 2048], P('ctx', 'tp')
- grad_post: bfloat16 [16384, 2048], P('ctx', 'tp')
- grad_pre: bfloat16 [16384, 2048], P('ctx', 'tp')
- grad_features: bfloat16 [16384, 2048], P('ctx', 'tp')
The draws below stay inside these ranges and needn't reach their ends.
All inputs are finite; a program needn't handle non-finite values.
Results may differ from the reference program's by a relative error of at most 0.022.
Values may be sent and summed in bfloat16 or wider, within the bound.
A program may use at most 128 MiB of HBM per device.

```python
import math
import jax
import jax.numpy as jnp
from jax import lax

FEATURE_HALF = 2048
DOUT = 2048
BASES = 4
SEQUENCE_LENGTH = 16384


def draw_filters(key, part):
    key = jax.random.fold_in(key, 7)
    generator_seeds = jax.random.split(key, 6)
    lag_shifts = jnp.arange(SEQUENCE_LENGTH, dtype=jnp.float32)[:, None]
    slow_share = 0.5
    slow_mask = jax.random.bernoulli(generator_seeds[0], slow_share, (FEATURE_HALF,))
    slow_rate = jnp.exp(jax.random.uniform(generator_seeds[1], (FEATURE_HALF,), jnp.float32, math.log(0.1 / SEQUENCE_LENGTH), math.log(1.0 / SEQUENCE_LENGTH)))
    fast_rate = jnp.exp(jax.random.uniform(generator_seeds[2], (FEATURE_HALF,), jnp.float32, math.log(1.0 / 50.0), math.log(1.0 / 30.0)))
    falloff_speed = jnp.where(slow_mask, slow_rate, fast_rate)[None, :]
    impulse_sites = jax.random.randint(generator_seeds[3], (2,), 1, SEQUENCE_LENGTH).astype(jnp.float32)
    impulse_weights = jax.random.uniform(generator_seeds[4], (2, FEATURE_HALF), jnp.float32, math.log(0.55), math.log(0.8))
    impulse_omission = jnp.where(lag_shifts >= impulse_sites[0], impulse_weights[0][None, :], 0.0)
    impulse_omission = impulse_omission + jnp.where(lag_shifts >= impulse_sites[1], impulse_weights[1][None, :], 0.0)
    filter_magnitude = jnp.sqrt(jnp.expm1(-2.0 * falloff_speed) / jnp.expm1(-2.0 * falloff_speed * SEQUENCE_LENGTH))
    noisy_component = jnp.clip(jax.random.normal(generator_seeds[5], (SEQUENCE_LENGTH, FEATURE_HALF), jnp.float32), -4.0, 4.0)
    return filter_magnitude * jnp.exp(impulse_omission - falloff_speed * lag_shifts) * noisy_component


def with_ends(array, key, least, high):
    longest = array.shape.index(max(array.shape))
    spots = []
    for shift in (0, 1):
        where = [jax.random.randint(jax.random.fold_in(key, axis), (), 0, length) for axis, length in enumerate(array.shape)]
        where[longest] = (where[longest] + shift) % array.shape[longest]
        spots.append(tuple(where))
    return array.at[spots[0]].set(least).at[spots[1]].set(high)


def steps_of(own_key, extent, shards, least, high):
    def one(axis_at, parts):
        steps = jax.random.uniform(jax.random.fold_in(jax.random.fold_in(own_key, 6), axis_at), (parts,), jnp.float32, least / len(shards), high / len(shards))
        return jnp.repeat(jnp.exp(steps), extent[axis_at] // parts).reshape((-1,) + (1,) * (len(extent) - axis_at - 1))

    loudness = one(*shards[0])
    for cut in shards[1:]:
        loudness = loudness * one(*cut)
    return loudness


def scatter_about(rng, dims, scale, bound, cuts=(), held_as=jnp.bfloat16):
    result = scale * jax.random.normal(rng, dims, jnp.float32)
    if cuts:
        result = result * steps_of(rng, dims, cuts, -0.22, 0.18)
    return jnp.clip(result, -bound, bound).astype(held_as)


def setup_inputs(seed: int = 0) -> dict:
    key_of = jax.random.split(jax.random.key(seed), 8)
    return {
        "post_gate": scatter_about(key_of[0], (SEQUENCE_LENGTH, FEATURE_HALF), 1.0, 6.0, ((0, 128), (1, 2))),
        "pre_gate": scatter_about(key_of[1], (SEQUENCE_LENGTH, FEATURE_HALF), 1.0, 6.0, ((0, 128), (1, 2))),
        "features": scatter_about(key_of[2], (SEQUENCE_LENGTH, FEATURE_HALF), 1.0, 6.0, ((0, 128), (1, 2))),
        "filters": draw_filters(jax.random.fold_in(key_of[7], 71), 0),
        "token_ids": with_ends(jax.random.randint(key_of[4], (SEQUENCE_LENGTH,), 0, BASES + 2), jax.random.fold_in(key_of[4], 1), 0, (BASES + 2) - 1).astype(jnp.int32),
        "out_weight": scatter_about(key_of[5], (FEATURE_HALF, DOUT), FEATURE_HALF ** -0.5, 0.125, ((0, 2),)),
        "out_grad": scatter_about(key_of[6], (SEQUENCE_LENGTH, DOUT), 1.0, 6.0, ((0, 128), (1, 2))),
    }


def causal_mix(signal, kernel, backward):
    length = 2 * signal.shape[0]
    signal_spec = jnp.fft.rfft(signal, n=length, axis=0)
    kernel_spec = jnp.fft.rfft(kernel, n=length, axis=0)
    if backward:
        kernel_spec = jnp.conj(kernel_spec)
    return jnp.fft.irfft(signal_spec * kernel_spec, n=length, axis=0)[: signal.shape[0]]


def grouped_mix(signal, kernel, backward):
    seq_len, channel_count = signal.shape
    group_width = math.gcd(channel_count, 256)
    group_count = channel_count // group_width
    signal_groups = signal.reshape(seq_len, group_count, group_width).transpose(1, 0, 2)
    kernel_groups = kernel.reshape(seq_len, group_count, group_width).transpose(1, 0, 2)

    def one_group(pair_args):
        return causal_mix(pair_args[0], pair_args[1], backward)

    mixed_groups = lax.map(one_group, (signal_groups, kernel_groups))
    return mixed_groups.transpose(1, 0, 2).reshape(seq_len, channel_count)


def reference(post_gate, pre_gate, features, filters, token_ids, out_weight, out_grad):
    keep_mask = (token_ids < BASES).astype(jnp.float32)[:, None]
    post_wide = post_gate.astype(jnp.float32)
    pre_wide = pre_gate.astype(jnp.float32)
    feat_wide = features.astype(jnp.float32)
    mixer_input = pre_wide * feat_wide * keep_mask
    mixed_signal = grouped_mix(mixer_input, filters, False)
    gated_out = (post_wide * mixed_signal).astype(jnp.bfloat16)
    output = jnp.dot(gated_out, out_weight, preferred_element_type=jnp.float32).astype(jnp.bfloat16)
    grad_gated = jnp.dot(out_grad, out_weight.T, preferred_element_type=jnp.float32)
    grad_post = (grad_gated * mixed_signal).astype(jnp.bfloat16)
    grad_mixed = grad_gated * post_wide
    grad_input = grouped_mix(grad_mixed, filters, True)
    grad_pre = (grad_input * feat_wide * keep_mask).astype(jnp.bfloat16)
    grad_features = (grad_input * pre_wide * keep_mask).astype(jnp.bfloat16)
    return output, grad_post, grad_pre, grad_features
```

```python
import math

import jax
import jax.numpy as jnp
import numpy as np
from jax import lax
from jax.experimental import pallas as pl
from jax.experimental.pallas import tpu as pltpu
from jax.sharding import PartitionSpec as P

BASES = 4
MESH = pl.DeviceIdType.MESH
F32 = jnp.float32
BF16 = jnp.bfloat16


def tables(n):
    steps = np.arange(n)
    outer = 2 * np.pi * ((2 * steps[:, None] + 1) * steps[None, :] % (4 * n)) / (4 * n)
    twist = 2 * np.pi * ((2 * steps[:, None] + 1) * steps[None, :]) / (4 * n * n)
    inner = 2 * np.pi * (steps[:, None] * steps[None, :] % n) / n
    c, s = np.cos(inner), np.sin(inner)
    as16 = lambda a: jnp.asarray(a.astype(np.float32)).astype(BF16)
    return (
        as16(np.concatenate([np.cos(outer), -np.sin(outer)], 0)),
        as16(np.block([[c, -s], [s, c]])),
        as16(np.block([[c, s], [-s, c]])),
        as16(np.concatenate([np.cos(outer).T, -np.sin(outer).T], 1) / (n * n)),
        jnp.asarray(np.cos(twist).astype(np.float32)),
        jnp.asarray(np.sin(twist).astype(np.float32)),
    )


def dot(a, b):
    return lax.dot_general(a, b, (((1,), (0,)), ((), ())), preferred_element_type=F32)


def dot_nt(a, b):
    return lax.dot_general(a, b, (((1,), (1,)), ((), ())), preferred_element_type=F32)


def kernel(
    post_ref, pre_ref, feat_ref, filt_ref, mask_ref, og_ref, w_hbm,
    f1_ref, m2_ref, m2i_ref, g1_ref, cos_ref, sin_ref,
    out_ref, gpost_ref, gpre_ref, gfeat_ref,
    w_ref, ogo_ref, xh_s, xh_r, g_s, g_r, y_s, y_r, gi_s, gi_r, part_s, part_r, mine_ref,
    grow_ref, gg_ref, wide_ref, back_ref, xs_ref, hs_ref,
    w_sem, s_sem, r_sem,
):
    n = lax.axis_size("ctx")
    me, tp = lax.axis_index("ctx"), lax.axis_index("tp")
    peer = 1 - tp
    tokens, channels = post_ref.shape
    own = channels // n
    cols = pl.ds(pl.multiple_of(tp * channels, channels), channels)
    peer_cols = pl.ds(pl.multiple_of(peer * channels, channels), channels)
    w_copy = pltpu.make_async_copy(w_hbm, w_ref, w_sem)
    w_copy.start()

    barrier = pltpu.get_barrier_semaphore()

    def greet(k, carry):
        pl.semaphore_signal(barrier, inc=1, device_id={"ctx": lax.rem(me + k, n)}, device_id_type=MESH)
        return carry

    lax.fori_loop(1, n, greet, 0)
    pl.semaphore_signal(barrier, inc=1, device_id={"tp": peer}, device_id_type=MESH)

    mask = mask_ref[...]
    per = 128 // own
    for k in range(channels // 128):
        at = slice(128 * k, 128 * k + 128)
        x = pre_ref[:, at].astype(F32) * feat_ref[:, at].astype(F32)
        x = (x.T * mask).reshape(per, own, tokens)
        h = filt_ref[:, at].T.reshape(per, own, tokens)
        xh_s[per * k : per * k + per] = jnp.concatenate([x, h], axis=1).astype(BF16)

    pl.semaphore_wait(barrier, n)

    def to_peer(src, dst, i):
        copy = pltpu.make_async_remote_copy(
            src_ref=src, dst_ref=dst, send_sem=s_sem.at[i], recv_sem=r_sem.at[i],
            device_id={"tp": peer}, device_id_type=MESH,
        )
        copy.start()
        return copy

    def to_all(src, dst, i):
        def go(k, carry):
            to = lax.rem(me + k, n)
            pltpu.make_async_remote_copy(
                src_ref=src.at[to], dst_ref=dst.at[me], send_sem=s_sem.at[i], recv_sem=r_sem.at[i],
                device_id={"ctx": to}, device_id_type=MESH,
            ).start()
            return carry

        lax.fori_loop(1, n, go, 0)
        dst[me] = src[me]
        return pltpu.make_async_remote_copy(
            src_ref=src.at[pl.ds(0, n - 1)], dst_ref=dst.at[pl.ds(0, n - 1)],
            send_sem=s_sem.at[i], recv_sem=r_sem.at[i],
            device_id={"ctx": lax.rem(me + 1, n)}, device_id_type=MESH,
        )

    og_copy = to_peer(og_ref, ogo_ref, 0)
    xh_copy = to_all(xh_s, xh_r, 1)

    w_copy.wait()
    gg_ref[...] = dot_nt(w_ref[:, cols], og_ref[...])
    og_copy.wait_recv()
    gg = gg_ref[...] + dot_nt(w_ref[:, peer_cols], ogo_ref[...])
    gg_ref[...] = gg
    for k in range(channels // 128):
        at = slice(128 * k, 128 * k + 128)
        g = gg_ref[at, :] * post_ref[:, at].astype(F32).T
        g_s[per * k : per * k + per] = g.reshape(per, own, tokens).astype(BF16)
    g_copy = to_all(g_s, g_r, 2)

    cos_t, sin_t = cos_ref[...], sin_ref[...]

    def spectrum(block):
        a = dot(f1_ref[...], block.astype(BF16))
        re, im = a[:n], a[n:]
        b = jnp.concatenate([re * cos_t + im * sin_t, im * cos_t - re * sin_t], axis=1)
        return dot(b.astype(BF16), m2_ref[...])

    def to_signal(re, im):
        d = dot(jnp.concatenate([re, im], axis=1).astype(BF16), m2i_ref[...])
        re, im = d[:, :tokens], d[:, tokens:]
        e = jnp.concatenate([re * cos_t - im * sin_t, im * cos_t + re * sin_t], axis=0)
        return dot(g1_ref[...], e.astype(BF16))

    xh_copy.wait_recv()
    wide_ref[...] = xh_r[...].astype(F32).reshape(n * 2 * own, tokens)
    for c in range(own):
        hs = spectrum(wide_ref[pl.ds(own + c, n, 2 * own), :])
        xs = spectrum(wide_ref[pl.ds(c, n, 2 * own), :])
        hs_ref[c] = hs
        hr, hi, xr, xi = hs[:, :tokens], hs[:, tokens:], xs[:, :tokens], xs[:, tokens:]
        back_ref[pl.ds(c, n, own), :] = to_signal(xr * hr - xi * hi, xr * hi + xi * hr)
    y_s[...] = back_ref[...].reshape(n, own, tokens).astype(BF16)
    y_copy = to_all(y_s, y_r, 3)

    g_copy.wait_recv()
    grow_ref[...] = g_r[...].astype(F32).reshape(n * own, tokens)
    for c in range(own):
        xs = spectrum(grow_ref[pl.ds(c, n, own), :])
        hs = hs_ref[c]
        hr, hi, xr, xi = hs[:, :tokens], hs[:, tokens:], xs[:, :tokens], xs[:, tokens:]
        back_ref[pl.ds(c, n, own), :] = to_signal(xr * hr + xi * hi, xi * hr - xr * hi)
    gi_s[...] = back_ref[...].reshape(n, own, tokens).astype(BF16)
    gi_copy = to_all(gi_s, gi_r, 4)

    y_copy.wait_recv()
    for k in range(channels // 128):
        at = slice(128 * k, 128 * k + 128)
        y = y_r[per * k : per * k + per].astype(F32).reshape(128, tokens)
        xs_ref[:, at] = (post_ref[:, at].astype(F32) * y.T).astype(BF16)
        gpost_ref[:, at] = (gg_ref[at, :] * y).T.astype(BF16)
    part_s[...] = dot(xs_ref[...], w_ref[:, peer_cols]).astype(BF16)
    part_copy = to_peer(part_s, part_r, 5)
    mine_ref[...] = dot(xs_ref[...], w_ref[:, cols])

    gi_copy.wait_recv()
    for k in range(channels // 128):
        at = slice(128 * k, 128 * k + 128)
        gi = gi_r[per * k : per * k + per].astype(F32).reshape(128, tokens)
        gi = (gi * mask).T
        gpre_ref[:, at] = (gi * feat_ref[:, at].astype(F32)).astype(BF16)
        gfeat_ref[:, at] = (gi * pre_ref[:, at].astype(F32)).astype(BF16)

    part_copy.wait_recv()
    out_ref[...] = (mine_ref[...] + part_r[...].astype(F32)).astype(BF16)
    for copy in (og_copy, xh_copy, g_copy, y_copy, gi_copy, part_copy):
        copy.wait_send()


def on_device(post_gate, pre_gate, features, filters, token_ids, out_weight, out_grad):
    tokens, channels = post_gate.shape
    n = lax.axis_size("ctx")
    own = channels // n
    keep = (token_ids < BASES).astype(F32)[None, :]
    vmem = pl.BlockSpec(memory_space=pltpu.VMEM)
    hbm = pl.BlockSpec(memory_space=pl.ANY)
    block = jax.ShapeDtypeStruct((tokens, channels), BF16)
    one = pltpu.VMEM((n, own, tokens), BF16)
    two = pltpu.VMEM((n, 2 * own, tokens), BF16)
    flat = pltpu.VMEM((tokens, channels), BF16)
    return pl.pallas_call(
        kernel,
        out_shape=(block,) * 4,
        in_specs=[vmem] * 6 + [hbm] + [vmem] * 6,
        out_specs=(vmem,) * 4,
        scratch_shapes=[
            pltpu.VMEM(out_weight.shape, BF16), flat, two, two, one, one, one, one, one, one, flat, flat,
            pltpu.VMEM((tokens, channels), F32),
            pltpu.VMEM((n * own, tokens), F32),
            pltpu.VMEM((channels, tokens), F32),
            pltpu.VMEM((n * 2 * own, tokens), F32),
            pltpu.VMEM((n * own, tokens), F32),
            flat,
            pltpu.VMEM((own, n, 2 * tokens), F32),
            pltpu.SemaphoreType.DMA,
            pltpu.SemaphoreType.DMA((6,)),
            pltpu.SemaphoreType.DMA((6,)),
        ],
        compiler_params=pltpu.CompilerParams(
            collective_id=0, has_side_effects=True, vmem_limit_bytes=48 * 2**20
        ),
    )(post_gate, pre_gate, features, filters, keep, out_grad, out_weight, *tables(tokens))


def solution(mesh):
    in_specs = (
        P("ctx", "tp"),
        P("ctx", "tp"),
        P("ctx", "tp"),
        P("ctx", "tp"),
        P("ctx"),
        P("tp", None),
        P("ctx", "tp"),
    )
    out_specs = (P("ctx", "tp"), P("ctx", "tp"), P("ctx", "tp"), P("ctx", "tp"))
    return jax.shard_map(
        on_device, mesh=mesh, in_specs=in_specs, out_specs=out_specs, check_vma=False
    )
```

```python
import math

import jax
import jax.numpy as jnp
import numpy as np
from jax import lax
from jax.experimental import pallas as pl
from jax.experimental.pallas import tpu as pltpu
from jax.sharding import PartitionSpec as P

BASES = 4
MESH = pl.DeviceIdType.MESH
F32 = jnp.float32
BF16 = jnp.bfloat16


def tables(n):
    steps = np.arange(n)
    outer = 2 * np.pi * ((2 * steps[:, None] + 1) * steps[None, :] % (4 * n)) / (4 * n)
    twist = 2 * np.pi * ((2 * steps[:, None] + 1) * steps[None, :]) / (4 * n * n)
    inner = 2 * np.pi * (steps[:, None] * steps[None, :] % n) / n
    c, s = np.cos(inner), np.sin(inner)
    first = np.concatenate([np.cos(outer), -np.sin(outer)], 0)
    coarse = first.astype(jnp.bfloat16).astype(np.float64)
    matrices = [
        np.concatenate([coarse, first - coarse], 1),
        np.block([[c, -s], [s, c]]),
        np.block([[c, s], [-s, c]]),
        np.concatenate([np.cos(outer).T, -np.sin(outer).T], 1) / (n * n),
    ]
    return (
        jnp.asarray(np.concatenate(matrices, 0).astype(np.float32)).astype(BF16),
        jnp.asarray(np.concatenate([np.cos(twist), np.sin(twist)], 0).astype(np.float32)),
    )


def dot(a, b):
    return lax.dot_general(a, b, (((1,), (0,)), ((), ())), preferred_element_type=F32)


def dot_nt(a, b):
    return lax.dot_general(a, b, (((1,), (1,)), ((), ())), preferred_element_type=F32)


def kernel(
    post_hbm, pre_hbm, feat_hbm, filt_hbm, ids_hbm, og_hbm, w_hbm, tab_hbm, twist_hbm,
    out_ref, gpost_ref, gpre_ref, gfeat_ref,
    post_ref, pre_ref, feat_ref, filt_ref, ids_ref, og_ref, w_ref, tab_ref, twist_ref,
    ogo_ref, h_s, h_r, x_s, x_r, g_s, g_r, y_s, y_r, gi_s, gi_r, part_s, part_r, mine_ref,
    gg_ref, flat_ref, rows_ref, mid_ref, hs_ref, xs_ref, e_ref, gated_ref,
    in_sem, s_sem, r_sem,
):
    n = lax.axis_size("ctx")
    me, tp = lax.axis_index("ctx"), lax.axis_index("tp")
    peer = 1 - tp
    tokens, channels = post_ref.shape
    own = channels // n
    loads = {}
    for i, (name, src, dst) in enumerate((
        ("pre", pre_hbm, pre_ref), ("feat", feat_hbm, feat_ref), ("ids", ids_hbm, ids_ref),
        ("filt", filt_hbm, filt_ref), ("og", og_hbm, og_ref), ("w", w_hbm, w_ref),
        ("post", post_hbm, post_ref), ("tab", tab_hbm, tab_ref), ("twist", twist_hbm, twist_ref),
    )):
        loads[name] = pltpu.make_async_copy(src, dst, in_sem.at[i])
        loads[name].start()
    cols = pl.ds(pl.multiple_of(tp * channels, channels), channels)
    peer_cols = pl.ds(pl.multiple_of(peer * channels, channels), channels)

    barrier = pltpu.get_barrier_semaphore()

    def greet(k, carry):
        pl.semaphore_signal(barrier, inc=1, device_id={"ctx": lax.rem(me + k, n)}, device_id_type=MESH)
        return carry

    lax.fori_loop(1, n, greet, 0)
    pl.semaphore_signal(barrier, inc=1, device_id={"tp": peer}, device_id_type=MESH)

    per = 128 // own
    slabs = channels // 128
    loads["filt"].wait()
    for k in range(slabs):
        h = filt_ref[:, 128 * k : 128 * k + 128].T
        h_s[per * k : per * k + per] = h.reshape(per, own, tokens).astype(BF16)

    pl.semaphore_wait(barrier, n)

    def to_peer(src, dst, i):
        copy = pltpu.make_async_remote_copy(
            src_ref=src, dst_ref=dst, send_sem=s_sem.at[i], recv_sem=r_sem.at[i],
            device_id={"tp": peer}, device_id_type=MESH,
        )
        copy.start()
        return copy

    def to_all(src, dst, i):
        def send(dy, dx, dz, dc):
            to = (
                lax.rem(me // 64 + dy, 2) * 64 + lax.rem(me // 16 + dx, 4) * 16
                + lax.rem(me // 2 + dz, 8) * 2 + lax.rem(me + dc, 2)
            )
            pltpu.make_async_remote_copy(
                src_ref=src.at[to], dst_ref=dst.at[me], send_sem=s_sem.at[i], recv_sem=r_sem.at[i],
                device_id={"ctx": to}, device_id_type=MESH,
            ).start()

        for group in ((4,), (3, 5), (2, 6), (1, 7)):
            def ring(p, carry):
                for dz in group:
                    send(lax.rem(p // 2 + 1, 2), lax.rem(6 - p // 4, 4), dz, lax.rem(p, 2))
                return carry

            lax.fori_loop(0, 16, ring, 0)

        def plane(p, carry):
            send(lax.rem(p // 2, 2), p // 4, 0, lax.rem(p, 2))
            return carry

        lax.fori_loop(1, 16, plane, 0)
        dst[me] = src[me]
        return pltpu.make_async_remote_copy(
            src_ref=src.at[pl.ds(0, n - 1)], dst_ref=dst.at[pl.ds(0, n - 1)],
            send_sem=s_sem.at[i], recv_sem=r_sem.at[i],
            device_id={"ctx": lax.rem(me + 1, n)}, device_id_type=MESH,
        )

    loads["og"].wait()
    og_copy = to_peer(og_ref, ogo_ref, 0)
    h_copy = to_all(h_s, h_r, 1)

    for name in ("pre", "feat", "ids"):
        loads[name].wait()
    mask = jnp.where(ids_ref[...] < BASES, 1.0, 0.0)
    for k in range(slabs):
        at = slice(128 * k, 128 * k + 128)
        x = pre_ref[:, at].astype(F32) * feat_ref[:, at].astype(F32)
        x_s[per * k : per * k + per] = (x.T * mask).reshape(per, own, tokens).astype(BF16)
    x_copy = to_all(x_s, x_r, 2)

    for name in ("w", "post", "tab", "twist"):
        loads[name].wait()
    gg_ref[...] = dot_nt(w_ref[:, cols], og_ref[...])
    og_copy.wait_recv()
    gg = gg_ref[...] + dot_nt(w_ref[:, peer_cols], ogo_ref[...])
    gg_ref[...] = gg
    for k in range(slabs):
        at = slice(128 * k, 128 * k + 128)
        g = gg_ref[at, :] * post_ref[:, at].astype(F32).T
        g_s[per * k : per * k + per] = g.reshape(per, own, tokens).astype(BF16)
    g_copy = to_all(g_s, g_r, 3)

    cos_t, sin_t = twist_ref[:n], twist_ref[n:]
    f1_ref, m2_ref, m2i_ref, g1_ref = (
        tab_ref.at[pl.ds(0, 2 * n)], tab_ref.at[pl.ds(2 * n, 2 * n)],
        tab_ref.at[pl.ds(4 * n, 2 * n)], tab_ref.at[pl.ds(6 * n, n)],
    )

    def spectra(received, result):
        flat_ref[...] = received[...].astype(F32).reshape(n * own, tokens)
        for c in range(own):
            block = flat_ref[pl.ds(c, n, own), :].astype(BF16)
            at = slice(tokens * c, tokens * c + tokens)
            rows_ref[:n, at] = block
            rows_ref[n:, at] = block
        for c in range(0, own, 2):
            a = dot(f1_ref[...], rows_ref[:, tokens * c : tokens * (c + 2)])
            for i in range(2):
                re, im = a[:n, tokens * i : tokens * (i + 1)], a[n:, tokens * i : tokens * (i + 1)]
                mid_ref[c + i, :, :tokens] = (re * cos_t + im * sin_t).astype(BF16)
                mid_ref[c + i, :, tokens:] = (im * cos_t - re * sin_t).astype(BF16)
        for c in range(own):
            result[c] = dot(mid_ref[c], m2_ref[...])

    def signals(sign, send):
        for c in range(own):
            hr, hi = hs_ref[c, :, :tokens], hs_ref[c, :, tokens:] * sign
            xr, xi = xs_ref[c, :, :tokens], xs_ref[c, :, tokens:]
            mid_ref[c, :, :tokens] = (xr * hr - xi * hi).astype(BF16)
            mid_ref[c, :, tokens:] = (xr * hi + xi * hr).astype(BF16)
        for c in range(own):
            at = slice(tokens * c, tokens * c + tokens)
            d = dot(mid_ref[c], m2i_ref[...])
            re, im = d[:, :tokens], d[:, tokens:]
            e_ref[:n, at] = (re * cos_t - im * sin_t).astype(BF16)
            e_ref[n:, at] = (im * cos_t + re * sin_t).astype(BF16)
        for c in range(0, own, 2):
            out = dot(g1_ref[...], e_ref[:, tokens * c : tokens * (c + 2)])
            for i in range(2):
                flat_ref[pl.ds(c + i, n, own), :] = out[:, tokens * i : tokens * (i + 1)]
        send[...] = flat_ref[...].reshape(n, own, tokens).astype(BF16)

    h_copy.wait_recv()
    spectra(h_r, hs_ref)
    x_copy.wait_recv()
    spectra(x_r, xs_ref)
    signals(1.0, y_s)
    y_copy = to_all(y_s, y_r, 4)

    g_copy.wait_recv()
    spectra(g_r, xs_ref)
    signals(-1.0, gi_s)
    gi_copy = to_all(gi_s, gi_r, 5)

    y_copy.wait_recv()
    for k in range(slabs):
        at = slice(128 * k, 128 * k + 128)
        y = y_r[per * k : per * k + per].astype(F32).reshape(128, tokens)
        gated_ref[:, at] = (post_ref[:, at].astype(F32) * y.T).astype(BF16)
    part_s[...] = dot(gated_ref[...], w_ref[:, peer_cols]).astype(BF16)
    part_copy = to_peer(part_s, part_r, 6)
    mine_ref[...] = dot(gated_ref[...], w_ref[:, cols])
    for k in range(slabs):
        at = slice(128 * k, 128 * k + 128)
        y = y_r[per * k : per * k + per].astype(F32).reshape(128, tokens)
        gpost_ref[:, at] = (gg_ref[at, :] * y).T.astype(BF16)

    gi_copy.wait_recv()
    for k in range(slabs):
        at = slice(128 * k, 128 * k + 128)
        gi = gi_r[per * k : per * k + per].astype(F32).reshape(128, tokens)
        gi = (gi * mask).T
        gpre_ref[:, at] = (gi * feat_ref[:, at].astype(F32)).astype(BF16)
        gfeat_ref[:, at] = (gi * pre_ref[:, at].astype(F32)).astype(BF16)

    part_copy.wait_recv()
    out_ref[...] = (mine_ref[...] + part_r[...].astype(F32)).astype(BF16)
    for copy in (og_copy, h_copy, x_copy, g_copy, y_copy, gi_copy, part_copy):
        copy.wait_send()


def store(*refs):
    sem = refs[-1]
    copies = [pltpu.make_async_copy(refs[i], refs[4 + i], sem.at[i]) for i in range(4)]
    for copy in copies:
        copy.start()
    for copy in copies:
        copy.wait()


def on_device(post_gate, pre_gate, features, filters, token_ids, out_weight, out_grad):
    tokens, channels = post_gate.shape
    n = lax.axis_size("ctx")
    own = channels // n
    vmem = pl.BlockSpec(memory_space=pltpu.VMEM)
    hbm = pl.BlockSpec(memory_space=pl.ANY)
    block = jax.ShapeDtypeStruct((tokens, channels), BF16)
    one = pltpu.VMEM((n, own, tokens), BF16)
    flat = pltpu.VMEM((tokens, channels), BF16)
    table, twist = tables(tokens)
    results = pl.pallas_call(
        kernel,
        out_shape=(block,) * 4,
        in_specs=[hbm] * 9,
        out_specs=(vmem,) * 4,
        scratch_shapes=[
            flat, flat, flat, pltpu.VMEM((tokens, channels), F32), pltpu.VMEM((1, tokens), jnp.int32), flat,
            pltpu.VMEM(out_weight.shape, BF16), pltpu.VMEM(table.shape, BF16), pltpu.VMEM(twist.shape, F32),
            flat, one, one, one, one, one, one, one, one, one, one, flat, flat,
            pltpu.VMEM((tokens, channels), F32),
            pltpu.VMEM((channels, tokens), F32),
            pltpu.VMEM((n * own, tokens), F32),
            pltpu.VMEM((2 * n, own * tokens), BF16),
            pltpu.VMEM((own, n, 2 * tokens), BF16),
            pltpu.VMEM((own, n, 2 * tokens), F32),
            pltpu.VMEM((own, n, 2 * tokens), F32),
            pltpu.VMEM((2 * n, own * tokens), BF16),
            flat,
            pltpu.SemaphoreType.DMA((9,)),
            pltpu.SemaphoreType.DMA((7,)),
            pltpu.SemaphoreType.DMA((7,)),
        ],
        compiler_params=pltpu.CompilerParams(
            collective_id=0, has_side_effects=True, vmem_limit_bytes=60 * 2**20
        ),
    )(post_gate, pre_gate, features, filters, token_ids.reshape(1, tokens), out_grad, out_weight, table, twist)
    return pl.pallas_call(
        store,
        out_shape=(block,) * 4,
        in_specs=[vmem] * 4,
        out_specs=(hbm,) * 4,
        scratch_shapes=[pltpu.SemaphoreType.DMA((4,))],
    )(*results)


def solution(mesh):
    in_specs = (
        P("ctx", "tp"),
        P("ctx", "tp"),
        P("ctx", "tp"),
        P("ctx", "tp"),
        P("ctx"),
        P("tp", None),
        P("ctx", "tp"),
    )
    out_specs = (P("ctx", "tp"), P("ctx", "tp"), P("ctx", "tp"), P("ctx", "tp"))
    return jax.shard_map(
        on_device, mesh=mesh, in_specs=in_specs, out_specs=out_specs, check_vma=False
    )
```

```python
import math

import jax
import jax.numpy as jnp
import numpy as np
from jax import lax
from jax.experimental import pallas as pl
from jax.experimental.pallas import tpu as pltpu
from jax.sharding import PartitionSpec as P

BASES = 4
MESH = pl.DeviceIdType.MESH
F32 = jnp.float32
BF16 = jnp.bfloat16


def tables(n):
    steps = np.arange(n)
    outer = 2 * np.pi * ((2 * steps[:, None] + 1) * steps[None, :] % (4 * n)) / (4 * n)
    twist = 2 * np.pi * ((2 * steps[:, None] + 1) * steps[None, :]) / (4 * n * n)
    inner = 2 * np.pi * (steps[:, None] * steps[None, :] % n) / n
    c, s = np.cos(inner), np.sin(inner)
    first = np.concatenate([np.cos(outer), -np.sin(outer)], 0)
    coarse = first.astype(jnp.bfloat16).astype(np.float64)
    matrices = [
        np.concatenate([coarse, first - coarse], 1),
        np.block([[c, -s], [s, c]]),
        np.block([[c, s], [-s, c]]),
        np.concatenate([np.cos(outer).T, -np.sin(outer).T], 1) / (n * n),
    ]
    return (
        jnp.asarray(np.concatenate(matrices, 0).astype(np.float32)).astype(BF16),
        jnp.asarray(np.concatenate([np.cos(twist), np.sin(twist)], 0).astype(np.float32)),
    )


def dot(a, b):
    return lax.dot_general(a, b, (((1,), (0,)), ((), ())), preferred_element_type=F32)


def dot_nt(a, b):
    return lax.dot_general(a, b, (((1,), (1,)), ((), ())), preferred_element_type=F32)


def kernel(
    post_hbm, pre_hbm, feat_hbm, filt_hbm, ids_hbm, og_hbm, w_hbm, tab_hbm, twist_hbm,
    out_ref, gpost_ref, gpre_ref, gfeat_ref,
    post_ref, pre_ref, feat_ref, filt_ref, ids_ref, og_ref, w_ref, tab_ref, twist_ref,
    ogo_ref, h_s, h_r, x_s, x_r, g_s, g_r, y_s, y_r, gi_s, gi_r, part_s, part_r, mine_ref,
    gg_ref, flat_ref, rows_ref, mid_ref, hs_ref, xs_ref, e_ref, gated_ref,
    in_sem, s_sem, r_sem, ring_sem,
):
    n = lax.axis_size("ctx")
    me, tp = lax.axis_index("ctx"), lax.axis_index("tp")
    peer = 1 - tp
    tokens, channels = post_ref.shape
    own = channels // n
    loads = {}
    for i, (name, src, dst) in enumerate((
        ("filt", filt_hbm, filt_ref), ("pre", pre_hbm, pre_ref), ("feat", feat_hbm, feat_ref),
        ("ids", ids_hbm, ids_ref), ("og", og_hbm, og_ref), ("w", w_hbm, w_ref),
        ("post", post_hbm, post_ref), ("tab", tab_hbm, tab_ref), ("twist", twist_hbm, twist_ref),
    )):
        loads[name] = pltpu.make_async_copy(src, dst, in_sem.at[i])

    def load(*names):
        for name in names:
            loads[name].start()

    load("filt", "pre", "feat", "ids", "og")
    cols = pl.ds(pl.multiple_of(tp * channels, channels), channels)
    peer_cols = pl.ds(pl.multiple_of(peer * channels, channels), channels)

    my_y, my_x, my_z, my_c = me // 64, lax.rem(me // 16, 4), lax.rem(me // 2, 8), lax.rem(me, 2)

    def at_offset(dy, dx, dz, dc):
        return (
            lax.rem(my_y + dy, 2) * 64 + lax.rem(my_x + dx, 4) * 16
            + lax.rem(my_z + dz, 8) * 2 + lax.rem(my_c + dc, 2)
        )

    barrier = pltpu.get_barrier_semaphore()

    def greet(semaphore, to):
        pl.semaphore_signal(semaphore, inc=1, device_id={"ctx": to}, device_id_type=MESH)

    for dz in range(1, 8):
        greet(barrier, at_offset(0, 0, dz, 0))
    for p in range(1, 16):
        greet(barrier, at_offset(p // 2 % 2, p // 4, 0, p % 2))
    pl.semaphore_signal(barrier, inc=1, device_id={"tp": peer}, device_id_type=MESH)

    per = 128 // own
    slabs = channels // 128
    loads["filt"].wait()
    for k in range(slabs):
        h = filt_ref[:, 128 * k : 128 * k + 128].T
        h_s[per * k : per * k + per] = h.reshape(per, own, tokens).astype(BF16)

    load("w", "post", "tab", "twist")
    pl.semaphore_wait(barrier, 23)
    for dz in range(1, 8):
        greet(ring_sem, at_offset(0, 0, dz, 0))

    def to_peer(src, dst, i):
        copy = pltpu.make_async_remote_copy(
            src_ref=src, dst_ref=dst, send_sem=s_sem.at[i], recv_sem=r_sem.at[i],
            device_id={"tp": peer}, device_id_type=MESH,
        )
        copy.start()
        return copy

    def to_half(src, dst, i, dy):
        def send(dx, dz, dc):
            to = at_offset(dy, dx, dz, dc)
            pltpu.make_async_remote_copy(
                src_ref=src.at[to], dst_ref=dst.at[me], send_sem=s_sem.at[i], recv_sem=r_sem.at[i],
                device_id={"ctx": to}, device_id_type=MESH,
            ).start()

        for group in ((4,), (3, 5), (2, 6), (1, 7)):
            def ring(p, carry):
                for dz in group:
                    send(lax.rem(6 - p // 2, 4), dz, lax.rem(p, 2))
                return carry

            lax.fori_loop(0, 8, ring, 0)

        def plane(p, carry):
            send(p // 2, 0, lax.rem(p, 2))
            return carry

        lax.fori_loop(1 - dy, 8, plane, 0)

    def all_of(src, dst, i):
        return pltpu.make_async_remote_copy(
            src_ref=src.at[pl.ds(0, n - 1)], dst_ref=dst.at[pl.ds(0, n - 1)],
            send_sem=s_sem.at[i], recv_sem=r_sem.at[i],
            device_id={"ctx": lax.rem(me + 1, n)}, device_id_type=MESH,
        )

    def to_all(src, dst, i):
        to_half(src, dst, i, 1)
        to_half(src, dst, i, 0)
        dst[me] = src[me]
        return all_of(src, dst, i)

    loads["og"].wait()
    og_copy = to_peer(og_ref, ogo_ref, 0)
    pl.semaphore_wait(ring_sem, 7)
    to_half(h_s, h_r, 1, 0)
    for name in ("pre", "feat", "ids"):
        loads[name].wait()
    mask = jnp.where(ids_ref[...] < BASES, 1.0, 0.0)
    for k in range(slabs):
        at = slice(128 * k, 128 * k + 128)
        x = pre_ref[:, at].astype(F32) * feat_ref[:, at].astype(F32)
        x_s[per * k : per * k + per] = (x.T * mask).reshape(per, own, tokens).astype(BF16)
    to_half(x_s, x_r, 2, 0)
    to_half(h_s, h_r, 1, 1)
    to_half(x_s, x_r, 2, 1)
    h_r[me] = h_s[me]
    x_r[me] = x_s[me]
    h_copy, x_copy = all_of(h_s, h_r, 1), all_of(x_s, x_r, 2)

    for name in ("w", "post", "tab", "twist"):
        loads[name].wait()
    gg_ref[...] = dot_nt(w_ref[:, cols], og_ref[...])
    og_copy.wait_recv()
    gg = gg_ref[...] + dot_nt(w_ref[:, peer_cols], ogo_ref[...])
    gg_ref[...] = gg
    for k in range(slabs):
        at = slice(128 * k, 128 * k + 128)
        g = gg_ref[at, :] * post_ref[:, at].astype(F32).T
        g_s[per * k : per * k + per] = g.reshape(per, own, tokens).astype(BF16)
    g_copy = to_all(g_s, g_r, 3)

    cos_t, sin_t = twist_ref[:n], twist_ref[n:]
    f1_ref, m2_ref, m2i_ref, g1_ref = (
        tab_ref.at[pl.ds(0, 2 * n)], tab_ref.at[pl.ds(2 * n, 2 * n)],
        tab_ref.at[pl.ds(4 * n, 2 * n)], tab_ref.at[pl.ds(6 * n, n)],
    )

    def spectra(received, result):
        flat_ref[...] = received[...].astype(F32).reshape(n * own, tokens)
        for c in range(own):
            block = flat_ref[pl.ds(c, n, own), :].astype(BF16)
            at = slice(tokens * c, tokens * c + tokens)
            rows_ref[:n, at] = block
            rows_ref[n:, at] = block
        for c in range(0, own, 2):
            a = dot(f1_ref[...], rows_ref[:, tokens * c : tokens * (c + 2)])
            for i in range(2):
                re, im = a[:n, tokens * i : tokens * (i + 1)], a[n:, tokens * i : tokens * (i + 1)]
                mid_ref[c + i, :, :tokens] = (re * cos_t + im * sin_t).astype(BF16)
                mid_ref[c + i, :, tokens:] = (im * cos_t - re * sin_t).astype(BF16)
        for c in range(own):
            result[c] = dot(mid_ref[c], m2_ref[...])

    def signals(sign, send):
        for c in range(own):
            hr, hi = hs_ref[c, :, :tokens], hs_ref[c, :, tokens:] * sign
            xr, xi = xs_ref[c, :, :tokens], xs_ref[c, :, tokens:]
            mid_ref[c, :, :tokens] = (xr * hr - xi * hi).astype(BF16)
            mid_ref[c, :, tokens:] = (xr * hi + xi * hr).astype(BF16)
        for c in range(own):
            at = slice(tokens * c, tokens * c + tokens)
            d = dot(mid_ref[c], m2i_ref[...])
            re, im = d[:, :tokens], d[:, tokens:]
            e_ref[:n, at] = (re * cos_t - im * sin_t).astype(BF16)
            e_ref[n:, at] = (im * cos_t + re * sin_t).astype(BF16)
        for c in range(0, own, 2):
            out = dot(g1_ref[...], e_ref[:, tokens * c : tokens * (c + 2)])
            for i in range(2):
                flat_ref[pl.ds(c + i, n, own), :] = out[:, tokens * i : tokens * (i + 1)]
        send[...] = flat_ref[...].reshape(n, own, tokens).astype(BF16)

    h_copy.wait_recv()
    spectra(h_r, hs_ref)
    x_copy.wait_recv()
    spectra(x_r, xs_ref)
    signals(1.0, y_s)
    y_copy = to_all(y_s, y_r, 4)

    g_copy.wait_recv()
    spectra(g_r, xs_ref)
    signals(-1.0, gi_s)
    gi_copy = to_all(gi_s, gi_r, 5)

    y_copy.wait_recv()
    for k in range(slabs):
        at = slice(128 * k, 128 * k + 128)
        y = y_r[per * k : per * k + per].astype(F32).reshape(128, tokens)
        gated_ref[:, at] = (post_ref[:, at].astype(F32) * y.T).astype(BF16)
    parts = []
    half = channels // 2
    for i in range(2):
        to = pl.ds(pl.multiple_of(peer * channels + i * half, half), half)
        part_s[i] = dot(gated_ref[...], w_ref[:, to]).astype(BF16)
        parts.append(to_peer(part_s.at[i], part_r.at[i], 6 + i))
    mine_ref[...] = dot(gated_ref[...], w_ref[:, cols])
    for k in range(slabs):
        at = slice(128 * k, 128 * k + 128)
        y = y_r[per * k : per * k + per].astype(F32).reshape(128, tokens)
        gpost_ref[:, at] = (gg_ref[at, :] * y).T.astype(BF16)

    gi_copy.wait_recv()
    for k in range(slabs):
        at = slice(128 * k, 128 * k + 128)
        gi = gi_r[per * k : per * k + per].astype(F32).reshape(128, tokens)
        gi = (gi * mask).T
        gpre_ref[:, at] = (gi * feat_ref[:, at].astype(F32)).astype(BF16)
        gfeat_ref[:, at] = (gi * pre_ref[:, at].astype(F32)).astype(BF16)

    for i, copy in enumerate(parts):
        at = slice(i * half, i * half + half)
        copy.wait_recv()
        out_ref[:, at] = (mine_ref[:, at] + part_r[i].astype(F32)).astype(BF16)
    for copy in (og_copy, h_copy, x_copy, g_copy, y_copy, gi_copy, *parts):
        copy.wait_send()


def store(*refs):
    sem = refs[-1]
    copies = [pltpu.make_async_copy(refs[i], refs[4 + i], sem.at[i]) for i in range(4)]
    for copy in copies:
        copy.start()
    for copy in copies:
        copy.wait()


def on_device(post_gate, pre_gate, features, filters, token_ids, out_weight, out_grad):
    tokens, channels = post_gate.shape
    n = lax.axis_size("ctx")
    own = channels // n
    vmem = pl.BlockSpec(memory_space=pltpu.VMEM)
    hbm = pl.BlockSpec(memory_space=pl.ANY)
    block = jax.ShapeDtypeStruct((tokens, channels), BF16)
    one = pltpu.VMEM((n, own, tokens), BF16)
    flat = pltpu.VMEM((tokens, channels), BF16)
    split = pltpu.VMEM((2, tokens, channels // 2), BF16)
    table, twist = tables(tokens)
    results = pl.pallas_call(
        kernel,
        out_shape=(pltpu.VMEM((tokens, channels), BF16),) * 4,
        in_specs=[hbm] * 9,
        out_specs=(vmem,) * 4,
        scratch_shapes=[
            flat, flat, flat, pltpu.VMEM((tokens, channels), F32), pltpu.VMEM((1, tokens), jnp.int32), flat,
            pltpu.VMEM(out_weight.shape, BF16), pltpu.VMEM(table.shape, BF16), pltpu.VMEM(twist.shape, F32),
            flat, one, one, one, one, one, one, one, one, one, one, split, split,
            pltpu.VMEM((tokens, channels), F32),
            pltpu.VMEM((channels, tokens), F32),
            pltpu.VMEM((n * own, tokens), F32),
            pltpu.VMEM((2 * n, own * tokens), BF16),
            pltpu.VMEM((own, n, 2 * tokens), BF16),
            pltpu.VMEM((own, n, 2 * tokens), F32),
            pltpu.VMEM((own, n, 2 * tokens), F32),
            pltpu.VMEM((2 * n, own * tokens), BF16),
            flat,
            pltpu.SemaphoreType.DMA((9,)),
            pltpu.SemaphoreType.DMA((8,)),
            pltpu.SemaphoreType.DMA((8,)),
            pltpu.SemaphoreType.REGULAR,
        ],
        compiler_params=pltpu.CompilerParams(
            collective_id=0, has_side_effects=True, vmem_limit_bytes=60 * 2**20
        ),
    )(post_gate, pre_gate, features, filters, token_ids.reshape(1, tokens), out_grad, out_weight, table, twist)
    return pl.pallas_call(
        store,
        out_shape=(block,) * 4,
        in_specs=[vmem] * 4,
        out_specs=(hbm,) * 4,
        compiler_params=pltpu.CompilerParams(vmem_limit_bytes=8 * 2**20),
        scratch_shapes=[pltpu.SemaphoreType.DMA((4,))],
    )(*results)


def solution(mesh):
    in_specs = (
        P("ctx", "tp"),
        P("ctx", "tp"),
        P("ctx", "tp"),
        P("ctx", "tp"),
        P("ctx"),
        P("tp", None),
        P("ctx", "tp"),
    )
    out_specs = (P("ctx", "tp"), P("ctx", "tp"), P("ctx", "tp"), P("ctx", "tp"))
    return jax.shard_map(
        on_device, mesh=mesh, in_specs=in_specs, out_specs=out_specs, check_vma=False
    )
```

```python
import math

import jax
import jax.numpy as jnp
import numpy as np
from jax import lax
from jax.experimental import pallas as pl
from jax.experimental.pallas import tpu as pltpu
from jax.sharding import PartitionSpec as P

BASES = 4
MESH = pl.DeviceIdType.MESH
F32 = jnp.float32
BF16 = jnp.bfloat16


def tables(n):
    steps = np.arange(n)
    outer = 2 * np.pi * ((2 * steps[:, None] + 1) * steps[None, :] % (4 * n)) / (4 * n)
    twist = 2 * np.pi * ((2 * steps[:, None] + 1) * steps[None, :]) / (4 * n * n)
    inner = 2 * np.pi * (steps[:, None] * steps[None, :] % n) / n
    c, s = np.cos(inner), np.sin(inner)
    first = np.concatenate([np.cos(outer), -np.sin(outer)], 0)
    coarse = first.astype(jnp.bfloat16).astype(np.float64)
    matrices = [
        np.concatenate([coarse, first - coarse], 1),
        np.block([[c, -s], [s, c]]),
        np.block([[c, s], [-s, c]]),
        np.concatenate([np.cos(outer).T, -np.sin(outer).T], 1) / (n * n),
    ]
    return (
        jnp.asarray(np.concatenate(matrices, 0).astype(np.float32)).astype(BF16),
        jnp.asarray(np.concatenate([np.cos(twist), np.sin(twist)], 0).astype(np.float32)),
    )


def dot(a, b):
    return lax.dot_general(a, b, (((1,), (0,)), ((), ())), preferred_element_type=F32)


def dot_nt(a, b):
    return lax.dot_general(a, b, (((1,), (1,)), ((), ())), preferred_element_type=F32)


def kernel(
    post_hbm, pre_hbm, feat_hbm, filt_hbm, ids_hbm, og_hbm, w_hbm, tab_hbm, twist_hbm,
    out_ref, gpost_ref, gpre_ref, gfeat_ref,
    post_ref, pre_ref, feat_ref, filt_ref, ids_ref, og_ref, w_ref, tab_ref, twist_ref,
    ogo_ref, h_s, h_r, x_s, x_r, g_s, g_r, y_s, y_r, gi_s, gi_r, gpeer_ref, wp_ref, mine_ref,
    gg_ref, flat_ref, rows_ref, mid_ref, hs_ref, xs_ref, e_ref, gated_ref,
    in_sem, s_sem, r_sem, ring_sem, ws_sem, wr_sem,
):
    n = lax.axis_size("ctx")
    me, tp = lax.axis_index("ctx"), lax.axis_index("tp")
    peer = 1 - tp
    tokens, channels = post_ref.shape
    own = channels // n
    loads = {}
    for i, (name, src, dst) in enumerate((
        ("filt", filt_hbm, filt_ref), ("pre", pre_hbm, pre_ref), ("feat", feat_hbm, feat_ref),
        ("ids", ids_hbm, ids_ref), ("og", og_hbm, og_ref), ("w", w_hbm, w_ref),
        ("post", post_hbm, post_ref), ("tab", tab_hbm, tab_ref), ("twist", twist_hbm, twist_ref),
    )):
        loads[name] = pltpu.make_async_copy(src, dst, in_sem.at[i])

    def load(*names):
        for name in names:
            loads[name].start()

    load("filt", "pre", "feat", "ids", "og")
    cols = pl.ds(pl.multiple_of(tp * channels, channels), channels)
    peer_cols = pl.ds(pl.multiple_of(peer * channels, channels), channels)

    my_y, my_x, my_z, my_c = me // 64, lax.rem(me // 16, 4), lax.rem(me // 2, 8), lax.rem(me, 2)

    def at_offset(dy, dx, dz, dc):
        return (
            lax.rem(my_y + dy, 2) * 64 + lax.rem(my_x + dx, 4) * 16
            + lax.rem(my_z + dz, 8) * 2 + lax.rem(my_c + dc, 2)
        )

    barrier = pltpu.get_barrier_semaphore()

    def greet(semaphore, to):
        pl.semaphore_signal(semaphore, inc=1, device_id={"ctx": to}, device_id_type=MESH)

    for dz in range(1, 8):
        greet(barrier, at_offset(0, 0, dz, 0))
    for p in range(1, 16):
        greet(barrier, at_offset(p // 2 % 2, p // 4, 0, p % 2))
    pl.semaphore_signal(barrier, inc=1, device_id={"tp": peer}, device_id_type=MESH)
    across = {"ctx": at_offset(1, 0, 0, 0), "tp": peer}
    pl.semaphore_signal(barrier, inc=1, device_id=across, device_id_type=MESH)

    pl.semaphore_wait(barrier, 24)
    for dz in range(1, 8):
        greet(ring_sem, at_offset(0, 0, dz, 0))
    load("w", "post", "tab", "twist")
    per = 128 // own
    slabs = channels // 128
    loads["filt"].wait()
    for k in range(slabs):
        h = filt_ref[:, 128 * k : 128 * k + 128].T
        h_s[per * k : per * k + per] = h.reshape(per, own, tokens).astype(BF16)


    def to_peer(src, dst, i):
        copy = pltpu.make_async_remote_copy(
            src_ref=src, dst_ref=dst, send_sem=s_sem.at[i], recv_sem=r_sem.at[i],
            device_id={"tp": peer}, device_id_type=MESH,
        )
        copy.start()
        return copy

    def to_half(src, dst, i, dy):
        def send(dx, dz, dc):
            to = at_offset(dy, dx, dz, dc)
            pltpu.make_async_remote_copy(
                src_ref=src.at[to], dst_ref=dst.at[me], send_sem=s_sem.at[i], recv_sem=r_sem.at[i],
                device_id={"ctx": to}, device_id_type=MESH,
            ).start()

        for group in ((4,), (3, 5), (2, 6), (1, 7)):
            def ring(p, carry):
                for dz in group:
                    send(lax.rem(6 - p // 2, 4), dz, lax.rem(p, 2))
                return carry

            lax.fori_loop(0, 8, ring, 0)

        def plane(p, carry):
            send(p // 2, 0, lax.rem(p, 2))
            return carry

        lax.fori_loop(1 - dy, 8, plane, 0)

    def all_of(src, dst, i, count):
        return pltpu.make_async_remote_copy(
            src_ref=src.at[pl.ds(0, count)], dst_ref=dst.at[pl.ds(0, count)],
            send_sem=s_sem.at[i], recv_sem=r_sem.at[i],
            device_id={"ctx": at_offset(0, 0, 0, 1)}, device_id_type=MESH,
        )

    def to_all(src, dst, i):
        to_half(src, dst, i, 1)
        to_half(src, dst, i, 0)
        dst[me] = src[me]
        return all_of(src, dst, i, n - 1)

    def rows_of(x, c, start=0, count=128):
        return pl.ds(pl.multiple_of((x * 2 + c) * 128 + start, 64), count)

    def pass_weight(src, rows, i, to):
        copy = pltpu.make_async_remote_copy(
            src_ref=src, dst_ref=wp_ref.at[rows], send_sem=ws_sem.at[i], recv_sem=wr_sem.at[i],
            device_id=to, device_id_type=MESH,
        )
        copy.start()
        return copy

    right, left = {"ctx": at_offset(0, 1, 0, 0)}, {"ctx": at_offset(0, 3, 0, 0)}
    left_x, right_x = lax.rem(my_x + 3, 4), lax.rem(my_x + 1, 4)
    mine = rows_of(my_x, my_c)

    loads["og"].wait()
    og_copy = to_peer(og_ref, ogo_ref, 0)
    pl.semaphore_wait(ring_sem, 7)
    to_half(h_s, h_r, 1, 0)
    for name in ("pre", "feat", "ids"):
        loads[name].wait()
    mask = jnp.where(ids_ref[...] < BASES, 1.0, 0.0)
    for k in range(slabs):
        at = slice(128 * k, 128 * k + 128)
        x = pre_ref[:, at].astype(F32) * feat_ref[:, at].astype(F32)
        x_s[per * k : per * k + per] = (x.T * mask).reshape(per, own, tokens).astype(BF16)
    to_half(x_s, x_r, 2, 0)
    to_half(h_s, h_r, 1, 1)
    to_half(x_s, x_r, 2, 1)
    h_r[me] = h_s[me]
    x_r[me] = x_s[me]
    h_copy, x_copy = all_of(h_s, h_r, 1, n - 1), all_of(x_s, x_r, 2, n - 1)

    for name in ("w", "post", "tab", "twist"):
        loads[name].wait()
    passed = [pass_weight(w_ref.at[mine, peer_cols], mine, 0, across)]
    gg_ref[...] = dot_nt(w_ref[:, cols], og_ref[...])
    og_copy.wait_recv()
    gg = gg_ref[...] + dot_nt(w_ref[:, peer_cols], ogo_ref[...])
    gg_ref[...] = gg
    for k in range(slabs):
        at = slice(128 * k, 128 * k + 128)
        g = gg_ref[at, :] * post_ref[:, at].astype(F32).T
        g_s[per * k : per * k + per] = g.reshape(per, own, tokens).astype(BF16)
    g_copy = to_all(g_s, g_r, 3)
    passed[0].wait_recv()
    passed.append(pass_weight(wp_ref.at[mine], mine, 1, right))
    passed.append(pass_weight(wp_ref.at[mine], mine, 2, left))

    cos_t, sin_t = twist_ref[:n], twist_ref[n:]
    f1_ref, m2_ref, m2i_ref, g1_ref = (
        tab_ref.at[pl.ds(0, 2 * n)], tab_ref.at[pl.ds(2 * n, 2 * n)],
        tab_ref.at[pl.ds(4 * n, 2 * n)], tab_ref.at[pl.ds(6 * n, n)],
    )

    def spectra(received, result):
        flat_ref[...] = received[...].astype(F32).reshape(n * own, tokens)
        for c in range(own):
            block = flat_ref[pl.ds(c, n, own), :].astype(BF16)
            at = slice(tokens * c, tokens * c + tokens)
            rows_ref[:n, at] = block
            rows_ref[n:, at] = block
        for c in range(0, own, 2):
            a = dot(f1_ref[...], rows_ref[:, tokens * c : tokens * (c + 2)])
            for i in range(2):
                re, im = a[:n, tokens * i : tokens * (i + 1)], a[n:, tokens * i : tokens * (i + 1)]
                mid_ref[c + i, :, :tokens] = (re * cos_t + im * sin_t).astype(BF16)
                mid_ref[c + i, :, tokens:] = (im * cos_t - re * sin_t).astype(BF16)
        for c in range(own):
            result[c] = dot(mid_ref[c], m2_ref[...])

    def signals(sign, send):
        for c in range(own):
            hr, hi = hs_ref[c, :, :tokens], hs_ref[c, :, tokens:] * sign
            xr, xi = xs_ref[c, :, :tokens], xs_ref[c, :, tokens:]
            mid_ref[c, :, :tokens] = (xr * hr - xi * hi).astype(BF16)
            mid_ref[c, :, tokens:] = (xr * hi + xi * hr).astype(BF16)
        for c in range(own):
            at = slice(tokens * c, tokens * c + tokens)
            d = dot(mid_ref[c], m2i_ref[...])
            re, im = d[:, :tokens], d[:, tokens:]
            e_ref[:n, at] = (re * cos_t - im * sin_t).astype(BF16)
            e_ref[n:, at] = (im * cos_t + re * sin_t).astype(BF16)
        for c in range(0, own, 2):
            out = dot(g1_ref[...], e_ref[:, tokens * c : tokens * (c + 2)])
            for i in range(2):
                flat_ref[pl.ds(c + i, n, own), :] = out[:, tokens * i : tokens * (i + 1)]
        send[...] = flat_ref[...].reshape(n, own, tokens).astype(BF16)

    h_copy.wait_recv()
    spectra(h_r, hs_ref)
    x_copy.wait_recv()
    spectra(x_r, xs_ref)
    signals(1.0, y_s)
    to_half(y_s, y_r, 4, 1)
    to_half(y_s, y_r, 6, 0)
    y_r[me] = y_s[me]
    y_copies = all_of(y_s, y_r, 4, n // 2), all_of(y_s, y_r, 6, n // 2 - 1)
    passed[1].wait_recv()
    passed[2].wait_recv()
    rows = rows_of(left_x, my_c, 0, 64)
    passed.append(pass_weight(wp_ref.at[rows], rows, 3, right))
    rows = rows_of(right_x, my_c, 64, 64)
    passed.append(pass_weight(wp_ref.at[rows], rows, 4, left))

    g_copy.wait_recv()
    spectra(g_r, xs_ref)
    signals(-1.0, gi_s)
    to_half(gi_s, gi_r, 5, 1)
    gi_r[me] = gi_s[me]
    gi_copy = all_of(gi_s, gi_r, 5, n - 1)

    passed[3].wait_recv()
    passed[4].wait_recv()
    for x in range(4):
        rows = rows_of(x, my_c)
        passed.append(pass_weight(wp_ref.at[rows], rows, 5 + x, {"ctx": at_offset(0, 0, 0, 1)}))

    half = channels // 2
    halves = 1 - my_y, my_y
    gated = []
    for i, which in enumerate(halves):
        y_copies[i].wait_recv()
        for k in range(slabs // 2):
            at = pl.ds(pl.multiple_of(which * half + 128 * k, 128), 128)
            y = y_r[pl.ds(which * (n // 2) + per * k, per)].astype(F32).reshape(128, tokens)
            gated_ref[i, :, 128 * k : 128 * k + 128] = (post_ref[:, at].astype(F32) * y.T).astype(BF16)
        gated.append(to_peer(gated_ref.at[i], gpeer_ref.at[i], 7 + i))
        if i == 0:
            to_half(gi_s, gi_r, 5, 0)
        rows = pl.ds(pl.multiple_of(which * half, half), half)
        term = dot(gated_ref[i], w_ref[rows, cols])
        mine_ref[...] = term if i == 0 else mine_ref[...] + term
    for k in range(slabs):
        at = slice(128 * k, 128 * k + 128)
        y = y_r[per * k : per * k + per].astype(F32).reshape(128, tokens)
        gpost_ref[:, at] = (gg_ref[at, :] * y).T.astype(BF16)
    for copy in passed[5:]:
        copy.wait_recv()

    gi_copy.wait_recv()
    for k in range(slabs):
        at = slice(128 * k, 128 * k + 128)
        gi = gi_r[per * k : per * k + per].astype(F32).reshape(128, tokens)
        gi = (gi * mask).T
        gpre_ref[:, at] = (gi * feat_ref[:, at].astype(F32)).astype(BF16)
        gfeat_ref[:, at] = (gi * pre_ref[:, at].astype(F32)).astype(BF16)

    for i, which in enumerate(halves):
        gated[i].wait_recv()
        rows = pl.ds(pl.multiple_of(which * half, half), half)
        term = mine_ref[...] + dot(gpeer_ref[i], wp_ref[rows, :])
        if i == 0:
            mine_ref[...] = term
        else:
            out_ref[...] = term.astype(BF16)
    for copy in (og_copy, h_copy, x_copy, g_copy, *y_copies, gi_copy, *gated, *passed):
        copy.wait_send()


def store(*refs):
    sem = refs[-1]
    copies = [pltpu.make_async_copy(refs[i], refs[4 + i], sem.at[i]) for i in range(4)]
    for copy in copies:
        copy.start()
    for copy in copies:
        copy.wait()


def on_device(post_gate, pre_gate, features, filters, token_ids, out_weight, out_grad):
    tokens, channels = post_gate.shape
    n = lax.axis_size("ctx")
    own = channels // n
    vmem = pl.BlockSpec(memory_space=pltpu.VMEM)
    hbm = pl.BlockSpec(memory_space=pl.ANY)
    block = jax.ShapeDtypeStruct((tokens, channels), BF16)
    one = pltpu.VMEM((n, own, tokens), BF16)
    flat = pltpu.VMEM((tokens, channels), BF16)
    split = pltpu.VMEM((2, tokens, channels // 2), BF16)
    table, twist = tables(tokens)
    results = pl.pallas_call(
        kernel,
        out_shape=(pltpu.VMEM((tokens, channels), BF16),) * 4,
        in_specs=[hbm] * 9,
        out_specs=(vmem,) * 4,
        scratch_shapes=[
            flat, flat, flat, pltpu.VMEM((tokens, channels), F32), pltpu.VMEM((1, tokens), jnp.int32), flat,
            pltpu.VMEM(out_weight.shape, BF16), pltpu.VMEM(table.shape, BF16), pltpu.VMEM(twist.shape, F32),
            flat, one, one, one, one, one, one, one, one, one, one, split,
            pltpu.VMEM((channels, channels), BF16),
            pltpu.VMEM((tokens, channels), F32),
            pltpu.VMEM((channels, tokens), F32),
            pltpu.VMEM((n * own, tokens), F32),
            pltpu.VMEM((2 * n, own * tokens), BF16),
            pltpu.VMEM((own, n, 2 * tokens), BF16),
            pltpu.VMEM((own, n, 2 * tokens), F32),
            pltpu.VMEM((own, n, 2 * tokens), F32),
            pltpu.VMEM((2 * n, own * tokens), BF16),
            split,
            pltpu.SemaphoreType.DMA((9,)),
            pltpu.SemaphoreType.DMA((9,)),
            pltpu.SemaphoreType.DMA((9,)),
            pltpu.SemaphoreType.REGULAR,
            pltpu.SemaphoreType.DMA((9,)),
            pltpu.SemaphoreType.DMA((9,)),
        ],
        compiler_params=pltpu.CompilerParams(
            collective_id=0, has_side_effects=True, vmem_limit_bytes=60 * 2**20
        ),
    )(post_gate, pre_gate, features, filters, token_ids.reshape(1, tokens), out_grad, out_weight, table, twist)
    return pl.pallas_call(
        store,
        out_shape=(block,) * 4,
        in_specs=[vmem] * 4,
        out_specs=(hbm,) * 4,
        compiler_params=pltpu.CompilerParams(vmem_limit_bytes=8 * 2**20),
        scratch_shapes=[pltpu.SemaphoreType.DMA((4,))],
    )(*results)


def solution(mesh):
    in_specs = (
        P("ctx", "tp"),
        P("ctx", "tp"),
        P("ctx", "tp"),
        P("ctx", "tp"),
        P("ctx"),
        P("tp", None),
        P("ctx", "tp"),
    )
    out_specs = (P("ctx", "tp"), P("ctx", "tp"), P("ctx", "tp"), P("ctx", "tp"))
    return jax.shard_map(
        on_device, mesh=mesh, in_specs=in_specs, out_specs=out_specs, check_vma=False
    )
```

```python
import math

import jax
import jax.numpy as jnp
import numpy as np
from jax import lax
from jax.experimental import pallas as pl
from jax.experimental.pallas import tpu as pltpu
from jax.sharding import PartitionSpec as P

BASES = 4
MESH = pl.DeviceIdType.MESH
F32 = jnp.float32
BF16 = jnp.bfloat16


def tables(n):
    steps = np.arange(n)
    outer = 2 * np.pi * ((2 * steps[:, None] + 1) * steps[None, :] % (4 * n)) / (4 * n)
    twist = 2 * np.pi * ((2 * steps[:, None] + 1) * steps[None, :]) / (4 * n * n)
    inner = 2 * np.pi * (steps[:, None] * steps[None, :] % n) / n
    c, s = np.cos(inner), np.sin(inner)
    first = np.concatenate([np.cos(outer), -np.sin(outer)], 0)
    coarse = first.astype(jnp.bfloat16).astype(np.float64)
    matrices = [
        np.concatenate([coarse, first - coarse], 1),
        np.block([[c, -s], [s, c]]),
        np.block([[c, s], [-s, c]]),
        np.concatenate([np.cos(outer).T, -np.sin(outer).T], 1) / (n * n),
    ]
    return (
        jnp.asarray(np.concatenate(matrices, 0).astype(np.float32)).astype(BF16),
        jnp.asarray(np.concatenate([np.cos(twist), np.sin(twist)], 0).astype(np.float32)),
    )


def dot(a, b):
    return lax.dot_general(a, b, (((1,), (0,)), ((), ())), preferred_element_type=F32)


def dot_nt(a, b):
    return lax.dot_general(a, b, (((1,), (1,)), ((), ())), preferred_element_type=F32)


def kernel(
    post_hbm, pre_hbm, feat_hbm, filt_hbm, ids_hbm, og_hbm, w_hbm, tab_hbm, twist_hbm,
    out_ref, gpost_ref, gpre_ref, gfeat_ref,
    post_ref, pre_ref, feat_ref, filt_ref, ids_ref, og_ref, w_ref, tab_ref, twist_ref,
    ogo_ref, h_s, h_r, x_s, x_r, g_s, g_r, y_s, y_r, gi_s, gi_r, gpeer_ref, wp_ref, mine_ref,
    gg_ref, flat_ref, rows_ref, mid_ref, hs_ref, xs_ref, e_ref, gated_ref,
    in_sem, s_sem, r_sem, ring_sem, ws_sem, wr_sem,
):
    n = lax.axis_size("ctx")
    me, tp = lax.axis_index("ctx"), lax.axis_index("tp")
    peer = 1 - tp
    tokens, channels = post_ref.shape
    own = channels // n
    loads = {}
    for i, (name, src, dst) in enumerate((
        ("filt", filt_hbm, filt_ref), ("pre", pre_hbm, pre_ref), ("feat", feat_hbm, feat_ref),
        ("ids", ids_hbm, ids_ref), ("og", og_hbm, og_ref), ("w", w_hbm, w_ref),
        ("post", post_hbm, post_ref), ("tab", tab_hbm, tab_ref), ("twist", twist_hbm, twist_ref),
    )):
        loads[name] = pltpu.make_async_copy(src, dst, in_sem.at[i])

    def load(*names):
        for name in names:
            loads[name].start()

    load("filt", "pre", "feat", "ids", "og")
    cols = pl.ds(pl.multiple_of(tp * channels, channels), channels)
    peer_cols = pl.ds(pl.multiple_of(peer * channels, channels), channels)

    my_y, my_x, my_z, my_c = me // 64, lax.rem(me // 16, 4), lax.rem(me // 2, 8), lax.rem(me, 2)

    def at_offset(dy, dx, dz, dc):
        return (
            lax.rem(my_y + dy, 2) * 64 + lax.rem(my_x + dx, 4) * 16
            + lax.rem(my_z + dz, 8) * 2 + lax.rem(my_c + dc, 2)
        )

    barrier = pltpu.get_barrier_semaphore()

    def greet(semaphore, to):
        pl.semaphore_signal(semaphore, inc=1, device_id={"ctx": to}, device_id_type=MESH)

    for dz in range(1, 8):
        greet(barrier, at_offset(0, 0, dz, 0))
    for p in range(1, 16):
        greet(barrier, at_offset(p // 2 % 2, p // 4, 0, p % 2))
    pl.semaphore_signal(barrier, inc=1, device_id={"tp": peer}, device_id_type=MESH)
    across = {"ctx": at_offset(1, 0, 0, 0), "tp": peer}
    pl.semaphore_signal(barrier, inc=1, device_id=across, device_id_type=MESH)

    pl.semaphore_wait(barrier, 24)
    for dz in range(1, 8):
        greet(ring_sem, at_offset(0, 0, dz, 0))
    load("w", "post", "tab", "twist")
    per = 128 // own
    slabs = channels // 128
    def to_peer(src, dst, i):
        copy = pltpu.make_async_remote_copy(
            src_ref=src, dst_ref=dst, send_sem=s_sem.at[i], recv_sem=r_sem.at[i],
            device_id={"tp": peer}, device_id_type=MESH,
        )
        copy.start()
        return copy

    loads["og"].wait()
    og_copy = to_peer(og_ref, ogo_ref, 0)
    loads["filt"].wait()
    for k in range(slabs):
        h = filt_ref[:, 128 * k : 128 * k + 128].astype(BF16).T
        h_s[per * k : per * k + per] = h.reshape(per, own, tokens)


    def to_half(src, dst, i, dy):
        def send(dx, dz, dc):
            to = at_offset(dy, dx, dz, dc)
            pltpu.make_async_remote_copy(
                src_ref=src.at[to], dst_ref=dst.at[me], send_sem=s_sem.at[i], recv_sem=r_sem.at[i],
                device_id={"ctx": to}, device_id_type=MESH,
            ).start()

        for group in ((4,), (3, 5), (2, 6), (1, 7)):
            def ring(p, carry):
                for dz in group:
                    send(lax.rem(6 - p // 2, 4), dz, lax.rem(p, 2))
                return carry

            lax.fori_loop(0, 8, ring, 0)

        def plane(p, carry):
            send(p // 2, 0, lax.rem(p, 2))
            return carry

        lax.fori_loop(1 - dy, 8, plane, 0)

    def all_of(src, dst, i, count):
        return pltpu.make_async_remote_copy(
            src_ref=src.at[pl.ds(0, count)], dst_ref=dst.at[pl.ds(0, count)],
            send_sem=s_sem.at[i], recv_sem=r_sem.at[i],
            device_id={"ctx": at_offset(0, 0, 0, 1)}, device_id_type=MESH,
        )

    def to_all(src, dst, i):
        to_half(src, dst, i, 1)
        to_half(src, dst, i, 0)
        dst[me] = src[me]
        return all_of(src, dst, i, n - 1)

    def rows_of(x, c, start=0, count=128):
        return pl.ds(pl.multiple_of((x * 2 + c) * 128 + start, 64), count)

    def pass_weight(src, rows, i, to):
        copy = pltpu.make_async_remote_copy(
            src_ref=src, dst_ref=wp_ref.at[rows], send_sem=ws_sem.at[i], recv_sem=wr_sem.at[i],
            device_id=to, device_id_type=MESH,
        )
        copy.start()
        return copy

    right, left = {"ctx": at_offset(0, 1, 0, 0)}, {"ctx": at_offset(0, 3, 0, 0)}
    left_x, right_x = lax.rem(my_x + 3, 4), lax.rem(my_x + 1, 4)
    mine = rows_of(my_x, my_c)

    pl.semaphore_wait(ring_sem, 7)
    to_half(h_s, h_r, 1, 0)
    for name in ("pre", "feat", "ids"):
        loads[name].wait()
    mask = jnp.where(ids_ref[...] < BASES, 1.0, 0.0)
    for k in range(slabs):
        at = slice(128 * k, 128 * k + 128)
        x = pre_ref[:, at].astype(F32) * feat_ref[:, at].astype(F32)
        x_s[per * k : per * k + per] = (x.astype(BF16).T.astype(F32) * mask).reshape(per, own, tokens).astype(BF16)
    to_half(x_s, x_r, 2, 0)
    to_half(h_s, h_r, 1, 1)
    to_half(x_s, x_r, 2, 1)
    h_r[me] = h_s[me]
    x_r[me] = x_s[me]
    h_copy, x_copy = all_of(h_s, h_r, 1, n - 1), all_of(x_s, x_r, 2, n - 1)

    for name in ("w", "post", "tab", "twist"):
        loads[name].wait()
    passed = [pass_weight(w_ref.at[mine, peer_cols], mine, 0, across)]
    gg_ref[...] = dot_nt(w_ref[:, cols], og_ref[...])
    og_copy.wait_recv()
    gg = gg_ref[...] + dot_nt(w_ref[:, peer_cols], ogo_ref[...])
    gg_ref[...] = gg
    for k in range(slabs):
        at = slice(128 * k, 128 * k + 128)
        g = gg_ref[at, :] * post_ref[:, at].T.astype(F32)
        g_s[per * k : per * k + per] = g.reshape(per, own, tokens).astype(BF16)
    g_copy = to_all(g_s, g_r, 3)
    passed[0].wait_recv()
    passed.append(pass_weight(wp_ref.at[mine], mine, 1, right))
    passed.append(pass_weight(wp_ref.at[mine], mine, 2, left))

    cos_t, sin_t = twist_ref[:n], twist_ref[n:]
    f1_ref, m2_ref, m2i_ref, g1_ref = (
        tab_ref.at[pl.ds(0, 2 * n)], tab_ref.at[pl.ds(2 * n, 2 * n)],
        tab_ref.at[pl.ds(4 * n, 2 * n)], tab_ref.at[pl.ds(6 * n, n)],
    )

    def spectra(received, result):
        flat_ref[...] = received[...].astype(F32).reshape(n * own, tokens)
        for c in range(own):
            block = flat_ref[pl.ds(c, n, own), :].astype(BF16)
            at = slice(tokens * c, tokens * c + tokens)
            rows_ref[:n, at] = block
            rows_ref[n:, at] = block
        for c in range(0, own, 2):
            a = dot(f1_ref[...], rows_ref[:, tokens * c : tokens * (c + 2)])
            for i in range(2):
                re, im = a[:n, tokens * i : tokens * (i + 1)], a[n:, tokens * i : tokens * (i + 1)]
                mid_ref[c + i, :, :tokens] = (re * cos_t + im * sin_t).astype(BF16)
                mid_ref[c + i, :, tokens:] = (im * cos_t - re * sin_t).astype(BF16)
        for c in range(own):
            result[c] = dot(mid_ref[c], m2_ref[...])

    def signals(sign, send):
        for c in range(own):
            hr, hi = hs_ref[c, :, :tokens], hs_ref[c, :, tokens:] * sign
            xr, xi = xs_ref[c, :, :tokens], xs_ref[c, :, tokens:]
            mid_ref[c, :, :tokens] = (xr * hr - xi * hi).astype(BF16)
            mid_ref[c, :, tokens:] = (xr * hi + xi * hr).astype(BF16)
        for c in range(own):
            at = slice(tokens * c, tokens * c + tokens)
            d = dot(mid_ref[c], m2i_ref[...])
            re, im = d[:, :tokens], d[:, tokens:]
            e_ref[:n, at] = (re * cos_t - im * sin_t).astype(BF16)
            e_ref[n:, at] = (im * cos_t + re * sin_t).astype(BF16)
        for c in range(0, own, 2):
            out = dot(g1_ref[...], e_ref[:, tokens * c : tokens * (c + 2)])
            for i in range(2):
                flat_ref[pl.ds(c + i, n, own), :] = out[:, tokens * i : tokens * (i + 1)]
        send[...] = flat_ref[...].reshape(n, own, tokens).astype(BF16)

    h_copy.wait_recv()
    spectra(h_r, hs_ref)
    x_copy.wait_recv()
    spectra(x_r, xs_ref)
    signals(1.0, y_s)
    to_half(y_s, y_r, 4, 1)
    to_half(y_s, y_r, 6, 0)
    y_r[me] = y_s[me]
    y_copies = all_of(y_s, y_r, 4, n // 2), all_of(y_s, y_r, 6, n // 2 - 1)
    passed[1].wait_recv()
    passed[2].wait_recv()
    rows = rows_of(left_x, my_c, 0, 64)
    passed.append(pass_weight(wp_ref.at[rows], rows, 3, right))
    rows = rows_of(right_x, my_c, 64, 64)
    passed.append(pass_weight(wp_ref.at[rows], rows, 4, left))

    g_copy.wait_recv()
    spectra(g_r, xs_ref)
    signals(-1.0, gi_s)
    to_half(gi_s, gi_r, 5, 1)
    gi_r[me] = gi_s[me]
    gi_copy = all_of(gi_s, gi_r, 5, n - 1)

    passed[3].wait_recv()
    passed[4].wait_recv()
    for x in range(4):
        rows = rows_of(x, my_c)
        passed.append(pass_weight(wp_ref.at[rows], rows, 5 + x, {"ctx": at_offset(0, 0, 0, 1)}))

    half = channels // 2
    halves = 1 - my_y, my_y
    gated = []
    for i, which in enumerate(halves):
        y_copies[i].wait_recv()
        for k in range(slabs // 2):
            at = pl.ds(pl.multiple_of(which * half + 128 * k, 128), 128)
            y = y_r[pl.ds(which * (n // 2) + per * k, per)].reshape(128, tokens).T
            gated_ref[i, :, 128 * k : 128 * k + 128] = (post_ref[:, at].astype(F32) * y.astype(F32)).astype(BF16)
        gated.append(to_peer(gated_ref.at[i], gpeer_ref.at[i], 7 + i))
        if i == 0:
            to_half(gi_s, gi_r, 5, 0)
        rows = pl.ds(pl.multiple_of(which * half, half), half)
        term = dot(gated_ref[i], w_ref[rows, cols])
        mine_ref[...] = term if i == 0 else mine_ref[...] + term
    for k in range(slabs):
        at = slice(128 * k, 128 * k + 128)
        y = y_r[per * k : per * k + per].astype(F32).reshape(128, tokens)
        gpost_ref[:, at] = (gg_ref[at, :] * y).astype(BF16).T
    for copy in passed[5:]:
        copy.wait_recv()

    gi_copy.wait_recv()
    for k in range(slabs):
        at = slice(128 * k, 128 * k + 128)
        gi = gi_r[per * k : per * k + per].astype(F32).reshape(128, tokens)
        gi = (gi * mask).astype(BF16).T.astype(F32)
        gpre_ref[:, at] = (gi * feat_ref[:, at].astype(F32)).astype(BF16)
        gfeat_ref[:, at] = (gi * pre_ref[:, at].astype(F32)).astype(BF16)

    for i, which in enumerate(halves):
        gated[i].wait_recv()
        rows = pl.ds(pl.multiple_of(which * half, half), half)
        term = mine_ref[...] + dot(gpeer_ref[i], wp_ref[rows, :])
        if i == 0:
            mine_ref[...] = term
        else:
            out_ref[...] = term.astype(BF16)
    for copy in (og_copy, h_copy, x_copy, g_copy, *y_copies, gi_copy, *gated, *passed):
        copy.wait_send()


def store(*refs):
    sem = refs[-1]
    copies = [pltpu.make_async_copy(refs[i], refs[4 + i], sem.at[i]) for i in range(4)]
    for copy in copies:
        copy.start()
    for copy in copies:
        copy.wait()


def on_device(post_gate, pre_gate, features, filters, token_ids, out_weight, out_grad):
    tokens, channels = post_gate.shape
    n = lax.axis_size("ctx")
    own = channels // n
    vmem = pl.BlockSpec(memory_space=pltpu.VMEM)
    hbm = pl.BlockSpec(memory_space=pl.ANY)
    block = jax.ShapeDtypeStruct((tokens, channels), BF16)
    one = pltpu.VMEM((n, own, tokens), BF16)
    flat = pltpu.VMEM((tokens, channels), BF16)
    split = pltpu.VMEM((2, tokens, channels // 2), BF16)
    table, twist = tables(tokens)
    results = pl.pallas_call(
        kernel,
        out_shape=(pltpu.VMEM((tokens, channels), BF16),) * 4,
        in_specs=[hbm] * 9,
        out_specs=(vmem,) * 4,
        scratch_shapes=[
            flat, flat, flat, pltpu.VMEM((tokens, channels), F32), pltpu.VMEM((1, tokens), jnp.int32), flat,
            pltpu.VMEM(out_weight.shape, BF16), pltpu.VMEM(table.shape, BF16), pltpu.VMEM(twist.shape, F32),
            flat, one, one, one, one, one, one, one, one, one, one, split,
            pltpu.VMEM((channels, channels), BF16),
            pltpu.VMEM((tokens, channels), F32),
            pltpu.VMEM((channels, tokens), F32),
            pltpu.VMEM((n * own, tokens), F32),
            pltpu.VMEM((2 * n, own * tokens), BF16),
            pltpu.VMEM((own, n, 2 * tokens), BF16),
            pltpu.VMEM((own, n, 2 * tokens), F32),
            pltpu.VMEM((own, n, 2 * tokens), F32),
            pltpu.VMEM((2 * n, own * tokens), BF16),
            split,
            pltpu.SemaphoreType.DMA((9,)),
            pltpu.SemaphoreType.DMA((9,)),
            pltpu.SemaphoreType.DMA((9,)),
            pltpu.SemaphoreType.REGULAR,
            pltpu.SemaphoreType.DMA((9,)),
            pltpu.SemaphoreType.DMA((9,)),
        ],
        compiler_params=pltpu.CompilerParams(
            collective_id=0, has_side_effects=True, vmem_limit_bytes=60 * 2**20
        ),
    )(post_gate, pre_gate, features, filters, token_ids.reshape(1, tokens), out_grad, out_weight, table, twist)
    return pl.pallas_call(
        store,
        out_shape=(block,) * 4,
        in_specs=[vmem] * 4,
        out_specs=(hbm,) * 4,
        compiler_params=pltpu.CompilerParams(vmem_limit_bytes=8 * 2**20),
        scratch_shapes=[pltpu.SemaphoreType.DMA((4,))],
    )(*results)


def solution(mesh):
    in_specs = (
        P("ctx", "tp"),
        P("ctx", "tp"),
        P("ctx", "tp"),
        P("ctx", "tp"),
        P("ctx"),
        P("tp", None),
        P("ctx", "tp"),
    )
    out_specs = (P("ctx", "tp"), P("ctx", "tp"), P("ctx", "tp"), P("ctx", "tp"))
    return jax.shard_map(
        on_device, mesh=mesh, in_specs=in_specs, out_specs=out_specs, check_vma=False
    )
```
